128 devices in a mesh: bx: 16 (over x, y_hi, core), by: 8 (over z, y_lo).
Axes of the slice: x: 4, y: 4 (y_hi: 2, y_lo: 2; y = y_hi * 2 + y_lo), z: 4, core: 2. Of those that a mesh axis runs over, the one named last changes fastest.
Arguments:
- snapshots: bfloat16 [64, 3, 81920], P(None, None, ('bx', 'by')), may hold values from -8 to 8
- previous_block_coefficients: bfloat16 [80, 31, 2, 16, 15360], P('by', None, None, 'bx'), may hold values from -8 to 8, as said below
- band_widths: int32 [8], replicated, may hold values from 1 to 10, 33 in all
Outputs:
- filtered: bfloat16 [64, 3, 81920], P(None, None, ('bx', 'by'))
The draws below stay inside these ranges and needn't reach their ends.
Inputs may be any that keep to these rules, and one draw needn't show every extreme that they name: `previous_block_coefficients`: rows of slots that no frequency uses hold arbitrary values.
All inputs are finite; a program needn't handle non-finite values.
Results may differ from the reference program's by a relative error of at most 0.0025.
The reference program's roundings to bfloat16 on the way count: a program that leaves them out, or rounds other values in their place, can miss the bound.
Values may be sent and summed in bfloat16 or wider, within the bound.
A program may use at most 128 MiB of HBM per device.

```python
import math
import jax
import jax.numpy as jnp
import numpy as np
from jax import lax

NT = 64
BLOCK_COUNT = 32
COMP = 3
FMAX = 10
NF = 33
NPTS = 81920
PC = 40
FREQ_SLOT_TOTAL = 80
GROUP_PAIR_COUNT = 15360
N_BX = 16
N_BY = 8


def coherent_shapes(key):
    return jax.random.normal(key, (4, COMP, NPTS), jnp.float32)


def draw_snapshots(key, part):
    shapes = coherent_shapes(key)
    key = jax.random.fold_in(key, 7)
    amp_key, random_noise_key = jax.random.split(key)
    amplitude = 0.6 * jax.random.normal(amp_key, (4, NT), jnp.float32)
    values = 0.8 * jax.random.normal(random_noise_key, (NT, COMP, NPTS), jnp.float32)
    for index in range(4):
        values = values + amplitude[index][:, None, None] * shapes[index][None]
    return jnp.clip(values, -8.0, 8.0).astype(jnp.bfloat16)


def draw_previous_block_coefficients(key, part):
    shapes = coherent_shapes(key).reshape(4, COMP, N_BX, N_BY, N_BX, PC).transpose(0, 4, 3, 1, 2, 5).reshape(4, -1)
    key = jax.random.fold_in(key, 13)
    coefficient_key, random_noise_key = jax.random.split(key)
    fourier_coefficients = 0.6 * jax.random.normal(coefficient_key, (FREQ_SLOT_TOTAL, BLOCK_COUNT - 1, 2, 4), jnp.float32)
    per_slot_keys = jax.random.split(random_noise_key, FREQ_SLOT_TOTAL)

    def one_slot(inputs):
        slot_key, slot_coef = inputs
        values = 0.8 * jax.random.normal(slot_key, (BLOCK_COUNT - 1, 2, shapes.shape[1]), jnp.float32)
        for index in range(4):
            values = values + slot_coef[:, :, index, None] * shapes[index][None, None]
        return jnp.clip(values, -8.0, 8.0)
    sampled_values = lax.map(one_slot, (per_slot_keys, fourier_coefficients))
    return sampled_values.reshape(FREQ_SLOT_TOTAL, BLOCK_COUNT - 1, 2, N_BX, GROUP_PAIR_COUNT).astype(jnp.bfloat16)


def profile(count, total, bound, skew):
    weights = [(1 << 20) // math.isqrt(standing ** skew) + 1 for standing in range(2, count + 1)]
    rest, given = total - bound - (count - 1), [1] * (count - 1)
    while rest > 0:
        movable = [i for i in range(count - 1) if given[i] < bound]
        whole, budget = sum([weights[i] for i in movable]), rest
        for i in movable:
            addition = min(bound - given[i], max(1, budget * weights[i] // whole), rest)
            given[i] = given[i] + addition
            rest = rest - addition
    return np.array([bound] + given)


def uneven_parts(stream_key, count, total, limit, skew):
    if count == 2:
        one = jax.random.randint(stream_key, (), max(1, total - limit), min(limit, total - 1) + 1)
        return jnp.stack([one, total - one])
    lengths = jnp.asarray(profile(count, total, limit, skew), jnp.int32)
    pairs = (count - 1) // 2
    donor, taker = lengths[1:1 + 2 * pairs:2], lengths[2:2 + 2 * pairs:2]
    room = jnp.minimum(donor - 1, limit - taker)
    moved = jax.random.randint(jax.random.fold_in(stream_key, 1), (pairs,), 0, 1 << 20) % (room + 1)
    lengths = lengths.at[1:1 + 2 * pairs:2].set(donor - moved).at[2:2 + 2 * pairs:2].set(taker + moved)
    return lengths[jax.random.permutation(jax.random.fold_in(stream_key, 2), count)]


def setup_inputs(seed: int = 0) -> dict:
    streams_of = jax.random.split(jax.random.key(seed), 4)
    snapshots = draw_snapshots(jax.random.fold_in(streams_of[3], 71), 0)
    previous_block_coefficients = draw_previous_block_coefficients(jax.random.fold_in(streams_of[3], 71), 0)
    band_widths = uneven_parts(streams_of[2], N_BY, NF, FMAX, 2).astype(jnp.int32)
    return {"snapshots": snapshots, "previous_block_coefficients": previous_block_coefficients, "band_widths": band_widths}


def trig_tables(freq, valid, n_time):
    times = jnp.arange(n_time, dtype=jnp.int32)
    turns = freq[..., None] * times % n_time
    angle = turns.astype(jnp.float32) * (2.0 * math.pi / n_time)
    window = 0.5 - 0.5 * jnp.cos(times.astype(jnp.float32) * (2.0 * math.pi / n_time))
    factor = math.sqrt(8.0 / (3.0 * n_time))
    waves = jnp.stack([jnp.cos(angle), -jnp.sin(angle)], -2)
    forward = waves * (factor * window) * valid[..., None, None]
    weight = jnp.where((freq == 0) | (2 * freq == n_time), 1.0, 2.0) / (factor * n_time) * valid
    inverse = waves * weight[..., None, None]
    return (forward.astype(jnp.bfloat16), inverse.astype(jnp.bfloat16))

def complex_coef(g_real, g_imag):
    first = jnp.stack([g_real, g_imag], -1)
    second = jnp.stack([-g_imag, g_real], -1)
    return jnp.stack([first, second], -2)

def reference(snapshots, previous_block_coefficients, band_widths):
    n_freq = NT // 2 + 1
    freq = jnp.arange(n_freq, dtype=jnp.int32)
    forward, inverse = trig_tables(freq, jnp.ones((n_freq,), jnp.float32), NT)
    points = snapshots.reshape(NT, COMP, N_BX, N_BY, N_BX, PC).transpose(0, 4, 3, 1, 2, 5).reshape(NT, -1)
    spectra = jnp.dot(forward.reshape(n_freq * 2, NT).astype(jnp.float32), points.astype(jnp.float32), preferred_element_type=jnp.float32)
    spectra = spectra.astype(jnp.bfloat16).reshape(n_freq, 2, -1)
    previous_all_blocks = previous_block_coefficients.reshape(FREQ_SLOT_TOTAL, BLOCK_COUNT - 1, 2, -1)
    ends = jnp.cumsum(band_widths).astype(jnp.int32)
    starts = (ends - band_widths).astype(jnp.int32)

    def one_frequency(index):
        band = jnp.sum((index >= ends).astype(jnp.int32)).astype(jnp.int32)
        slot = (band * FMAX + index - starts[band]).astype(jnp.int32)
        old_rows = lax.dynamic_index_in_dim(previous_all_blocks, slot, 0, keepdims=False)
        new_rows = lax.dynamic_index_in_dim(spectra, index, 0, keepdims=False)
        blocks = jnp.concatenate([old_rows, new_rows[None]], 0).reshape(2 * BLOCK_COUNT, -1)
        prod = jnp.dot(blocks.astype(jnp.float32), blocks.T.astype(jnp.float32), preferred_element_type=jnp.float32).reshape(BLOCK_COUNT, 2, BLOCK_COUNT, 2)
        m_real = prod[:, 0, :, 0] + prod[:, 1, :, 1]
        m_imag = prod[:, 0, :, 1] - prod[:, 1, :, 0]
        shift = jnp.trace(m_real) / BLOCK_COUNT
        shifted = m_real + shift * jnp.eye(BLOCK_COUNT, dtype=jnp.float32)
        system = jnp.concatenate([jnp.concatenate([shifted, -m_imag], 1), jnp.concatenate([m_imag, shifted], 1)], 0)
        target = jnp.concatenate([m_real[:, -1], m_imag[:, -1]], 0)
        solved = jnp.linalg.solve(system, target)
        g_real = solved[:BLOCK_COUNT].astype(jnp.bfloat16)
        g_imag = solved[BLOCK_COUNT:].astype(jnp.bfloat16)
        coef = complex_coef(g_real, g_imag).reshape(2 * BLOCK_COUNT, 2)
        rebuilt = jnp.dot(coef.T.astype(jnp.float32), blocks.astype(jnp.float32), preferred_element_type=jnp.float32)
        return rebuilt.astype(jnp.bfloat16)
    rebuilt_all = lax.map(one_frequency, freq)
    inverse_rows = inverse.reshape(n_freq * 2, NT).T
    result = jnp.dot(inverse_rows.astype(jnp.float32), rebuilt_all.reshape(n_freq * 2, -1).astype(jnp.float32), preferred_element_type=jnp.float32)
    result = result.astype(jnp.bfloat16)
    return result.reshape(NT, N_BX, N_BY, COMP, N_BX, PC).transpose(0, 3, 4, 2, 1, 5).reshape(NT, COMP, -1)
```

```python
import math

import jax
import jax.numpy as jnp
import ml_dtypes
import numpy as np
from jax import lax
from jax.experimental import pallas as pl
from jax.experimental.pallas import tpu as pltpu
from jax.sharding import PartitionSpec as P

MESH = pl.DeviceIdType.MESH
LANES = 128


def trig_constants(n_time):
    n_freq = n_time // 2 + 1
    freq = np.arange(n_freq, dtype=np.int32)
    times = np.arange(n_time, dtype=np.int32)
    turns = freq[:, None] * times % n_time
    angle = turns.astype(np.float32) * np.float32(2.0 * math.pi / n_time)
    window = np.float32(0.5) - np.float32(0.5) * np.cos(
        times.astype(np.float32) * np.float32(2.0 * math.pi / n_time)
    )
    factor = math.sqrt(8.0 / (3.0 * n_time))
    waves = np.stack([np.cos(angle), -np.sin(angle)], -2)
    forward = waves * (np.float32(factor) * window)
    weight = np.where((freq == 0) | (2 * freq == n_time), 1.0, 2.0) / (factor * n_time)
    inverse = waves * weight.astype(np.float32)[:, None, None]
    rows = 2 * n_freq
    table_f = np.zeros((LANES, n_time), np.float32)
    table_i = np.zeros((n_time, LANES), np.float32)
    table_f[:rows] = forward.reshape(rows, n_time)
    table_i[:, :rows] = inverse.reshape(rows, n_time).T
    return table_f.astype(ml_dtypes.bfloat16), table_i.astype(ml_dtypes.bfloat16)


def iota(shape, dim):
    return lax.broadcasted_iota(jnp.int32, shape, dim)


def place(acc, tile, dst, src, width, lane):
    shift = (dst - src) % LANES
    moved = pltpu.roll(tile, shift, 1) if shift else tile
    return jnp.where((lane >= dst) & (lane < dst + width), moved, acc)


def split_groups(tiles, n_comp, n_group, width):
    shape = tiles[0][0].shape
    lane = iota(shape, 1)
    out = []
    for s in range(n_group):
        acc = jnp.zeros(shape, jnp.float32)
        for k in range(n_comp):
            a, done = s * width, 0
            while done < width:
                t, off = (a + done) // LANES, (a + done) % LANES
                n = min(width - done, LANES - off)
                acc = place(acc, tiles[k][t], k * width + done, off, n, lane)
                done += n
        out.append(acc)
    return out


def merge_groups(tile_of, n_comp, n_group, width):
    loaded = [tile_of(s) for s in range(n_group)]
    shape = loaded[0].shape
    lane = iota(shape, 1)
    out = []
    for k in range(n_comp):
        row = []
        for t in range(n_group * width // LANES):
            acc = jnp.zeros(shape, jnp.float32)
            for s in range(t * LANES // width, (t * LANES + LANES - 1) // width + 1):
                lo = max(0, s * width - t * LANES)
                hi = min(LANES, (s + 1) * width - t * LANES)
                skip = lo - (s * width - t * LANES)
                acc = place(acc, loaded[s], lo, k * width + skip, hi - lo, lane)
            row.append(acc)
        out.append(row)
    return out


def kernel(
    n_bx, n_by, width,
    bw_ref, table_f_ref, table_i_ref, snap_ref, old_ref, out_ref,
    buf, acc, tx1, rx1, tx2, gtx, grx, htx, hrx, tx3, rx3, tx4, rx4,
    old_sem, own_sem, s1, r1, s2, r2, s3, r3, s4, r4, s5, r5, s6, r6,
):
    f32, bf16 = jnp.float32, jnp.bfloat16
    c, j = lax.axis_index("bx"), lax.axis_index("by")
    n_comp, n_time, p_local = snap_ref.shape
    slots, n_old = old_ref.shape[:2]
    n_all = 2 * (n_old + 1)
    per_comp = p_local // LANES
    chunk = n_comp * per_comp

    def old_copy(f, b):
        return pltpu.make_async_copy(old_ref.at[f, b], buf.at[:, f, b], old_sem.at[f])

    def start_old(n, carry):
        old_copy(n // n_old, n % n_old).start()
        return carry

    lax.fori_loop(0, slots * n_old, start_old, 0)

    barrier = pltpu.get_barrier_semaphore()

    def greet_bx(d, carry):
        pl.semaphore_signal(
            barrier, inc=1, device_id={"bx": lax.rem(c + d, n_bx)}, device_id_type=MESH
        )
        return carry

    def greet_by(d, carry):
        pl.semaphore_signal(
            barrier, inc=1, device_id={"by": lax.rem(j + d, n_by)}, device_id_type=MESH
        )
        return carry

    lax.fori_loop(1, n_bx, greet_bx, 0)
    lax.fori_loop(1, n_by, greet_by, 0)

    tiles = [
        [snap_ref[k, :, t * LANES : (t + 1) * LANES].astype(f32) for t in range(per_comp)]
        for k in range(n_comp)
    ]
    for s, tile in enumerate(split_groups(tiles, n_comp, n_bx, width)):
        tx1[s] = tile.astype(bf16)

    pl.semaphore_wait(barrier, n_bx + n_by - 2)

    def copy1(p, at):
        return pltpu.make_async_remote_copy(
            src_ref=tx1.at[p], dst_ref=rx1.at[at], send_sem=s1.at[p], recv_sem=r1.at[at],
            device_id={"bx": p}, device_id_type=MESH,
        )

    def send1(d, carry):
        copy1(lax.rem(c + d, n_bx), c).start()
        return carry

    lax.fori_loop(1, n_bx, send1, 0)
    rx1[c] = tx1[c]

    n_rows = n_by * slots * 2
    row = iota((n_rows, LANES), 0)
    col = iota((n_rows, LANES), 1)
    band = row // (2 * slots)
    slot = (row // 2) % slots
    start = jnp.int32(0)
    wanted = jnp.full((n_rows, LANES), -1, jnp.int32)
    for b in range(n_by):
        w = bw_ref[b]
        wanted = jnp.where((band == b) & (slot < w), 2 * (start + slot) + row % 2, wanted)
        start = start + w
    pick = jnp.where(col == wanted, 1.0, 0.0).astype(bf16)
    forward = jnp.dot(pick, table_f_ref[...], preferred_element_type=f32).astype(bf16)
    inverse = lax.dot_general(
        table_i_ref[...], pick, (((1,), (1,)), ((), ())), preferred_element_type=f32
    ).astype(bf16)

    def wait1(d, carry):
        copy1(c, lax.rem(c + n_bx - d, n_bx)).wait_recv()
        return carry

    lax.fori_loop(1, n_bx, wait1, 0)

    tx2_rows = tx2.reshape(chunk, n_rows, LANES)
    merged = merge_groups(lambda s: rx1[s].astype(f32), n_comp, n_bx, width)
    for k in range(n_comp):
        for t in range(per_comp):
            spectra = jnp.dot(forward, merged[k][t].astype(bf16), preferred_element_type=f32)
            tx2_rows[k * per_comp + t] = spectra.astype(bf16)

    def copy2(p, at):
        return pltpu.make_async_remote_copy(
            src_ref=tx2.at[:, pl.ds(p * slots, slots)],
            dst_ref=buf.at[pl.ds(at * chunk, chunk), :, n_old],
            send_sem=s2.at[p], recv_sem=r2.at[at],
            device_id={"by": p}, device_id_type=MESH,
        )

    def send2(d, carry):
        copy2(lax.rem(j + d, n_by), j).start()
        return carry

    lax.fori_loop(1, n_by, send2, 0)
    own = pltpu.make_async_copy(
        tx2.at[:, pl.ds(j * slots, slots)], buf.at[pl.ds(j * chunk, chunk), :, n_old], own_sem
    )
    own.start()

    def wait_old(f, carry):
        whole = buf.at[:, f, pl.ds(0, n_old)]
        pltpu.make_async_copy(whole, whole, old_sem.at[f]).wait()
        return carry

    lax.fori_loop(0, slots, wait_old, 0)
    own.wait()

    rows = buf.reshape(n_by * chunk, slots * n_all, LANES)

    def gram(p, first):
        for f in range(slots):
            x = jnp.concatenate(
                [rows[p * chunk + l, f * n_all : (f + 1) * n_all, :] for l in range(chunk)], 1
            )
            g = lax.dot_general(x, x, (((1,), (1,)), ((), ())), preferred_element_type=f32)
            if first:
                acc[f] = g
            else:
                acc[f] += g

    gram(j, True)

    def gram_step(d, carry):
        p = lax.rem(j + n_by - d, n_by)
        copy2(j, p).wait_recv()
        gram(p, False)
        return carry

    lax.fori_loop(1, n_by, gram_step, 0)

    half = n_all // 2
    for f in range(slots):
        g = acc[f]
        gtx[f] = jnp.concatenate([g[:half], g[half:]], 1)

    def copy3(p, at):
        return pltpu.make_async_remote_copy(
            src_ref=gtx.at[p], dst_ref=grx.at[at], send_sem=s3.at[p], recv_sem=r3.at[at],
            device_id={"bx": p}, device_id_type=MESH,
        )

    def each_other(n, fn):
        def step(d, carry):
            fn(d)
            return carry

        lax.fori_loop(1, n, step, 0)

    def send3(d):
        p = lax.rem(c + d, n_bx)

        @pl.when(p < slots)
        def _():
            copy3(p, c).start()

    each_other(n_bx, send3)

    def copy4(p, at):
        return pltpu.make_async_remote_copy(
            src_ref=htx, dst_ref=hrx.at[at], send_sem=s4.at[p], recv_sem=r4.at[at],
            device_id={"bx": p}, device_id_type=MESH,
        )

    @pl.when(c < slots)
    def _():
        grx[c] = gtx[c]
        each_other(n_bx, lambda d: copy3(c, lax.rem(c + n_bx - d, n_bx)).wait_recv())
        total = grx[0]
        for i in range(1, n_bx):
            total = total + grx[i]
        prod = jnp.concatenate([total, pltpu.roll(total, half * 2, 1)], 0)
        shape = prod.shape
        r, l = iota(shape, 0), iota(shape, 1)
        prod = jnp.where(l < n_all, prod, 0.0)
        swap = jnp.where(r % 2 == 0, pltpu.roll(prod, n_all - 1, 0), pltpu.roll(prod, 1, 0))
        swap = jnp.where(l % 2 == 0, pltpu.roll(swap, LANES - 1, 1), pltpu.roll(swap, 1, 1))
        m = prod + jnp.where((r + l) % 2 == 0, swap, -swap)
        valid = c < bw_ref[j]
        m = jnp.where(valid, m, 0.0)
        diagonal = r == l
        shift = jnp.sum(jnp.where(diagonal, m, 0.0)) / n_all + jnp.where(valid, 0.0, 1.0)
        system = jnp.where(diagonal, m + shift, m)
        system = jnp.where(
            l < n_all, system, jnp.where(l < n_all + 2, pltpu.roll(m, 2, 1), 0.0)
        )
        for p in range(n_old + 1):
            e = 2 * p
            inv = 1.0 / system[e : e + 1, e : e + 1]
            first, second = system[e : e + 1] * inv, system[e + 1 : e + 2] * inv
            left = system - system[:, e : e + 1] * first - system[:, e + 1 : e + 2] * second
            system = jnp.where(r == e, first, jnp.where(r == e + 1, second, left))
        turned = jnp.transpose(system)
        x0, x1 = turned[n_all : n_all + 1], turned[n_all + 1 : n_all + 2]
        x0, x1 = jnp.concatenate([x0, x0], 1), jnp.concatenate([x1, x1], 1)
        r8 = iota((8, LANES), 0)
        message = jnp.where(r8 == 0, x0, jnp.where(r8 == 1, x1, 0.0))
        htx[...] = message
        hrx[c] = message
        each_other(n_bx, lambda d: copy4(lax.rem(c + d, n_bx), c).start())

    def wait4(d):
        p = lax.rem(c + n_bx - d, n_bx)

        @pl.when(p < slots)
        def _():
            copy4(c, p).wait_recv()

    each_other(n_bx, wait4)

    w_rows = 32
    r, l = iota((w_rows, LANES), 0), iota((w_rows, LANES), 1)
    coef = []
    for t in range(slots // 2):
        even, odd = (
            jnp.where(r % 2 == 0, hrx[2 * t + u, 0:1, :], hrx[2 * t + u, 1:2, :])
            for u in range(2)
        )
        tile = jnp.where((r // 2 == 2 * t) & (l < n_all), even, 0.0)
        coef.append(jnp.where((r // 2 == 2 * t + 1) & (l >= n_all), odd, tile).astype(bf16))
    coef = jnp.concatenate(coef, 1)

    tx3_rows = tx3.reshape(n_by, chunk, 2 * slots, LANES)

    def rebuild(p):
        x = jnp.concatenate([rows[p * chunk + n] for n in range(chunk)], 1)
        y = jnp.dot(coef, x, preferred_element_type=f32)[: 2 * slots].astype(bf16)
        for n in range(chunk):
            tx3_rows[p, n] = y[:, n * LANES : (n + 1) * LANES]

    def copy5(p, at):
        return pltpu.make_async_remote_copy(
            src_ref=tx3.at[p], dst_ref=rx3.at[:, at], send_sem=s5.at[p], recv_sem=r5.at[at],
            device_id={"by": p}, device_id_type=MESH,
        )

    def send5(d):
        p = lax.rem(j + d, n_by)
        rebuild(p)
        copy5(p, j).start()

    each_other(n_by, send5)
    rebuild(j)
    own5 = pltpu.make_async_copy(tx3.at[j], rx3.at[:, j], own_sem)
    own5.start()
    own5.wait()
    each_other(n_by, lambda d: copy5(j, lax.rem(j + n_by - d, n_by)).wait_recv())

    rx3_rows = rx3.reshape(chunk, n_rows, LANES)
    tiles = [
        [
            jnp.dot(inverse, rx3_rows[k * per_comp + t], preferred_element_type=f32)
            .astype(bf16)
            .astype(f32)
            for t in range(per_comp)
        ]
        for k in range(n_comp)
    ]
    for s, tile in enumerate(split_groups(tiles, n_comp, n_bx, width)):
        tx4[s] = tile.astype(bf16)

    def copy6(p, at):
        return pltpu.make_async_remote_copy(
            src_ref=tx4.at[p], dst_ref=rx4.at[at], send_sem=s6.at[p], recv_sem=r6.at[at],
            device_id={"bx": p}, device_id_type=MESH,
        )

    each_other(n_bx, lambda d: copy6(lax.rem(c + d, n_bx), c).start())
    rx4[c] = tx4[c]
    each_other(n_bx, lambda d: copy6(c, lax.rem(c + n_bx - d, n_bx)).wait_recv())
    merged = merge_groups(lambda s: rx4[s].astype(f32), n_comp, n_bx, width)
    for k in range(n_comp):
        for t in range(per_comp):
            out_ref[k, :, t * LANES : (t + 1) * LANES] = merged[k][t].astype(bf16)

    def drain_bx(d):
        p = lax.rem(c + d, n_bx)
        copy1(p, c).wait_send()
        copy6(p, c).wait_send()

        @pl.when(p < slots)
        def _():
            copy3(p, c).wait_send()

        @pl.when(c < slots)
        def _():
            copy4(p, c).wait_send()

    def drain_by(d):
        p = lax.rem(j + d, n_by)
        copy2(p, j).wait_send()
        copy5(p, j).wait_send()

    each_other(n_bx, drain_bx)
    each_other(n_by, drain_by)


def local(snapshots, previous_block_coefficients, band_widths):
    n_time, n_comp, p_local = snapshots.shape
    n_bx = lax.axis_size("bx")
    n_by = lax.axis_size("by")
    slots, n_old = previous_block_coefficients.shape[:2]
    pairs = previous_block_coefficients.shape[-1]
    width = p_local // n_bx
    n_all = 2 * (n_old + 1)
    chunk = n_comp * p_local // LANES
    old = previous_block_coefficients.reshape(slots, n_old, 2, pairs // LANES, LANES)
    old = old.transpose(0, 1, 3, 2, 4)
    snap = snapshots.transpose(1, 0, 2)
    table_f, table_i = trig_constants(n_time)
    f32, bf16 = jnp.float32, jnp.bfloat16
    dma = pltpu.SemaphoreType.DMA
    vmem = pl.BlockSpec(memory_space=pltpu.VMEM)

    def body(*refs):
        kernel(n_bx, n_by, width, *refs)

    out = pl.pallas_call(
        body,
        out_shape=jax.ShapeDtypeStruct((n_comp, n_time, p_local), bf16),
        in_specs=[
            pl.BlockSpec(memory_space=pltpu.SMEM), vmem, vmem, vmem,
            pl.BlockSpec(memory_space=pl.ANY),
        ],
        out_specs=vmem,
        scratch_shapes=[
            pltpu.VMEM((pairs // LANES, slots, n_old + 1, 2, LANES), bf16),
            pltpu.VMEM((slots, n_all, n_all), f32),
            pltpu.VMEM((n_bx, n_time, LANES), bf16),
            pltpu.VMEM((n_bx, n_time, LANES), bf16),
            pltpu.VMEM((chunk, n_by * slots, 2, LANES), bf16),
            pltpu.VMEM((slots, n_all // 2, LANES), f32),
            pltpu.VMEM((n_bx, n_all // 2, LANES), f32),
            pltpu.VMEM((8, LANES), f32),
            pltpu.VMEM((slots, 8, LANES), f32),
            pltpu.VMEM((n_by, chunk, slots, 2, LANES), bf16),
            pltpu.VMEM((chunk, n_by, slots, 2, LANES), bf16),
            pltpu.VMEM((n_bx, n_time, LANES), bf16),
            pltpu.VMEM((n_bx, n_time, LANES), bf16),
            dma((slots,)), dma,
            dma((n_bx,)), dma((n_bx,)),
            dma((n_by,)), dma((n_by,)),
            dma((n_bx,)), dma((n_bx,)),
            dma((n_bx,)), dma((n_bx,)),
            dma((n_by,)), dma((n_by,)),
            dma((n_bx,)), dma((n_bx,)),
        ],
        compiler_params=pltpu.CompilerParams(
            collective_id=0, has_side_effects=True, vmem_limit_bytes=48 * 2**20
        ),
        cost_estimate=pl.CostEstimate(
            flops=4 * 10**9, bytes_accessed=20 * 10**6, transcendentals=0
        ),
    )(band_widths, jnp.asarray(table_f), jnp.asarray(table_i), snap, old)
    return out.transpose(1, 0, 2)


def solution(mesh):
    placed = (P(None, None, ("bx", "by")), P("by", None, None, "bx", None), P())
    return jax.shard_map(
        local, mesh=mesh, in_specs=placed, out_specs=P(None, None, ("bx", "by")), check_vma=False
    )
```

```python
import math

import jax
import jax.numpy as jnp
import ml_dtypes
import numpy as np
from jax import lax
from jax.experimental import pallas as pl
from jax.experimental.pallas import tpu as pltpu
from jax.sharding import PartitionSpec as P

MESH = pl.DeviceIdType.MESH
LANES = 128


def trig_constants(n_time):
    n_freq = n_time // 2 + 1
    freq = np.arange(n_freq, dtype=np.int32)
    times = np.arange(n_time, dtype=np.int32)
    turns = freq[:, None] * times % n_time
    angle = turns.astype(np.float32) * np.float32(2.0 * math.pi / n_time)
    window = np.float32(0.5) - np.float32(0.5) * np.cos(
        times.astype(np.float32) * np.float32(2.0 * math.pi / n_time)
    )
    factor = math.sqrt(8.0 / (3.0 * n_time))
    waves = np.stack([np.cos(angle), -np.sin(angle)], -2)
    forward = waves * (np.float32(factor) * window)
    weight = np.where((freq == 0) | (2 * freq == n_time), 1.0, 2.0) / (factor * n_time)
    inverse = waves * weight.astype(np.float32)[:, None, None]
    rows = 2 * n_freq
    table_f = np.zeros((LANES, n_time), np.float32)
    table_i = np.zeros((n_time, LANES), np.float32)
    table_f[:rows] = forward.reshape(rows, n_time)
    table_i[:, :rows] = inverse.reshape(rows, n_time).T
    return table_f.astype(ml_dtypes.bfloat16), table_i.astype(ml_dtypes.bfloat16)


def iota(shape, dim):
    return lax.broadcasted_iota(jnp.int32, shape, dim)


def place(acc, tile, dst, src, width, lane):
    shift = (dst - src) % LANES
    moved = pltpu.roll(tile, shift, 1) if shift else tile
    return jnp.where((lane >= dst) & (lane < dst + width), moved, acc)


def split_groups(tiles, n_comp, n_group, width):
    shape = tiles[0][0].shape
    lane = iota(shape, 1)
    out = []
    for s in range(n_group):
        acc = jnp.zeros(shape, jnp.float32)
        for k in range(n_comp):
            a, done = s * width, 0
            while done < width:
                t, off = (a + done) // LANES, (a + done) % LANES
                n = min(width - done, LANES - off)
                acc = place(acc, tiles[k][t], k * width + done, off, n, lane)
                done += n
        out.append(acc)
    return out


def merge_groups(tile_of, n_comp, n_group, width):
    loaded = [tile_of(s) for s in range(n_group)]
    shape = loaded[0].shape
    lane = iota(shape, 1)
    out = []
    for k in range(n_comp):
        row = []
        for t in range(n_group * width // LANES):
            acc = jnp.zeros(shape, jnp.float32)
            for s in range(t * LANES // width, (t * LANES + LANES - 1) // width + 1):
                lo = max(0, s * width - t * LANES)
                hi = min(LANES, (s + 1) * width - t * LANES)
                skip = lo - (s * width - t * LANES)
                acc = place(acc, loaded[s], lo, k * width + skip, hi - lo, lane)
            row.append(acc)
        out.append(row)
    return out


def kernel(
    n_bx, n_by, width,
    bw_ref, table_f_hbm, table_i_hbm, snap_hbm, old_ref, out_ref,
    snap_ref, table_f_ref, table_i_ref, buf, acc, tx1, rx1, tx2, gtx, grx, htx, hrx, tx3, rx3, tx4, rx4,
    snap_sem, table_sem, old_sem, own_sem, s1, r1, s2, r2, s3, r3, s4, r4, s5, r5, s6, r6,
):
    f32, bf16 = jnp.float32, jnp.bfloat16
    c, j = lax.axis_index("bx"), lax.axis_index("by")
    n_comp, n_time, p_local = snap_ref.shape
    slots, n_old = old_ref.shape[:2]
    n_all = 2 * (n_old + 1)
    per_comp = p_local // LANES
    chunk = n_comp * per_comp

    snap_copy = pltpu.make_async_copy(snap_hbm, snap_ref, snap_sem)
    snap_copy.start()
    table_copies = (
        pltpu.make_async_copy(table_f_hbm, table_f_ref, table_sem.at[0]),
        pltpu.make_async_copy(table_i_hbm, table_i_ref, table_sem.at[1]),
    )
    for copy in table_copies:
        copy.start()

    def each_other(n, fn):
        def step(d, carry):
            fn(d)
            return carry

        lax.fori_loop(1, n, step, 0)

    def arrived(*refs):
        for ref, sem in refs:
            pltpu.make_async_copy(ref, ref, sem).wait()

    barrier = pltpu.get_barrier_semaphore()

    def greet_bx(d, carry):
        pl.semaphore_signal(
            barrier, inc=1, device_id={"bx": lax.rem(c + d, n_bx)}, device_id_type=MESH
        )
        return carry

    def greet_by(d, carry):
        pl.semaphore_signal(
            barrier, inc=1, device_id={"by": lax.rem(j + d, n_by)}, device_id_type=MESH
        )
        return carry

    lax.fori_loop(1, n_bx, greet_bx, 0)
    lax.fori_loop(1, n_by, greet_by, 0)

    snap_copy.wait()
    tiles = [
        [snap_ref[k, :, t * LANES : (t + 1) * LANES].astype(f32) for t in range(per_comp)]
        for k in range(n_comp)
    ]
    for s, tile in enumerate(split_groups(tiles, n_comp, n_bx, width)):
        tx1[s] = tile.astype(bf16)

    pl.semaphore_wait(barrier, n_bx + n_by - 2)

    def copy1(p, at):
        return pltpu.make_async_remote_copy(
            src_ref=tx1.at[p], dst_ref=rx1.at[at], send_sem=s1, recv_sem=r1,
            device_id={"bx": p}, device_id_type=MESH,
        )

    def send1(d, carry):
        copy1(lax.rem(c + d, n_bx), c).start()
        return carry

    lax.fori_loop(1, n_bx, send1, 0)
    rx1[c] = tx1[c]

    def old_copy(f, b):
        return pltpu.make_async_copy(
            old_ref.at[f, b], buf.at[:, f, pl.ds(2 * b, 2)], old_sem.at[f]
        )

    def start_old(n, carry):
        old_copy(n // n_old, n % n_old).start()
        return carry

    lax.fori_loop(0, slots * n_old, start_old, 0)
    for copy in table_copies:
        copy.wait()

    n_rows = n_by * slots * 2
    row = iota((n_rows, LANES), 0)
    col = iota((n_rows, LANES), 1)
    band = row // (2 * slots)
    slot = (row // 2) % slots
    start = jnp.int32(0)
    wanted = jnp.full((n_rows, LANES), -1, jnp.int32)
    for b in range(n_by):
        w = bw_ref[b]
        wanted = jnp.where((band == b) & (slot < w), 2 * (start + slot) + row % 2, wanted)
        start = start + w
    pick = jnp.where(col == wanted, 1.0, 0.0).astype(bf16)
    forward = jnp.dot(pick, table_f_ref[...], preferred_element_type=f32).astype(bf16)
    inverse = lax.dot_general(
        table_i_ref[...], pick, (((1,), (1,)), ((), ())), preferred_element_type=f32
    ).astype(bf16)

    arrived((rx1.at[: n_bx - 1], r1))

    tx2_rows = tx2.reshape(chunk, n_rows, LANES)
    merged = merge_groups(lambda s: rx1[s].astype(f32), n_comp, n_bx, width)
    for k in range(n_comp):
        for t in range(per_comp):
            spectra = jnp.dot(forward, merged[k][t].astype(bf16), preferred_element_type=f32)
            tx2_rows[k * per_comp + t] = spectra.astype(bf16)

    part = slots // 2

    def copy2(p, at, h):
        return pltpu.make_async_remote_copy(
            src_ref=tx2.at[:, pl.ds(p * slots + h * part, part)],
            dst_ref=buf.at[pl.ds(at * chunk, chunk), pl.ds(h * part, part), pl.ds(2 * n_old, 2)],
            send_sem=s2, recv_sem=r2.at[h, at],
            device_id={"by": p}, device_id_type=MESH,
        )

    for h in range(2):
        each_other(n_by, lambda d: copy2(lax.rem(j + d, n_by), j, h).start())
    own = pltpu.make_async_copy(
        tx2.at[:, pl.ds(j * slots, slots)],
        buf.at[pl.ds(j * chunk, chunk), :, pl.ds(2 * n_old, 2)],
        own_sem,
    )
    own.start()

    def wait_old(f, carry):
        whole = buf.at[:, f, pl.ds(0, 2 * n_old)]
        pltpu.make_async_copy(whole, whole, old_sem.at[f]).wait()
        return carry

    lax.fori_loop(0, slots, wait_old, 0)
    own.wait()

    rows = buf.reshape(n_by * chunk, slots * n_all, LANES)
    half = n_all // 2

    def gram(p, h, first):
        for f in range(h * part, (h + 1) * part):
            x = jnp.concatenate(
                [rows[p * chunk + l, f * n_all : (f + 1) * n_all, :] for l in range(chunk)], 1
            )
            g = lax.dot_general(x, x, (((1,), (1,)), ((), ())), preferred_element_type=f32)
            if first:
                acc[f] = g
            else:
                acc[f] += g

    def copy3(p, at):
        return pltpu.make_async_remote_copy(
            src_ref=gtx.at[p], dst_ref=grx.at[at], send_sem=s3, recv_sem=r3,
            device_id={"bx": p}, device_id_type=MESH,
        )

    for h in range(2):
        gram(j, h, True)

        def gram_step(d):
            p = lax.rem(j + n_by - d, n_by)
            copy2(j, p, h).wait_recv()
            gram(p, h, False)

        each_other(n_by, gram_step)
        for f in range(h * part, (h + 1) * part):
            g = acc[f]
            gtx[f] = jnp.concatenate([g[:half], g[half:]], 1)

        def send3(d):
            p = lax.rem(c + d, n_bx)

            @pl.when((p >= h * part) & (p < (h + 1) * part))
            def _():
                copy3(p, c).start()

        each_other(n_bx, send3)

    def copy4(p, at):
        return pltpu.make_async_remote_copy(
            src_ref=htx, dst_ref=hrx.at[at], send_sem=s4, recv_sem=r4,
            device_id={"bx": p}, device_id_type=MESH,
        )

    @pl.when(c < slots)
    def _():
        grx[c] = gtx[c]
        arrived((grx.at[: n_bx - 1], r3))
        total = grx[0]
        for i in range(1, n_bx):
            total = total + grx[i]
        prod = jnp.concatenate([total, pltpu.roll(total, half * 2, 1)], 0)
        shape = prod.shape
        r, l = iota(shape, 0), iota(shape, 1)
        prod = jnp.where(l < n_all, prod, 0.0)
        swap = jnp.where(r % 2 == 0, pltpu.roll(prod, n_all - 1, 0), pltpu.roll(prod, 1, 0))
        swap = jnp.where(l % 2 == 0, pltpu.roll(swap, LANES - 1, 1), pltpu.roll(swap, 1, 1))
        m = prod + jnp.where((r + l) % 2 == 0, swap, -swap)
        valid = c < bw_ref[j]
        m = jnp.where(valid, m, 0.0)
        diagonal = r == l
        shift = jnp.sum(jnp.where(diagonal, m, 0.0)) / n_all + jnp.where(valid, 0.0, 1.0)
        system = jnp.where(diagonal, m + shift, m)
        system = jnp.where(
            l < n_all, system, jnp.where(l < n_all + 2, pltpu.roll(m, 2, 1), 0.0)
        )
        for p in range(n_old + 1):
            e = 2 * p
            inv = 1.0 / system[e : e + 1, e : e + 1]
            first, second = system[e : e + 1] * inv, system[e + 1 : e + 2] * inv
            left = system - system[:, e : e + 1] * first - system[:, e + 1 : e + 2] * second
            system = jnp.where(r == e, first, jnp.where(r == e + 1, second, left))
        turned = jnp.transpose(system)
        x0, x1 = turned[n_all : n_all + 1], turned[n_all + 1 : n_all + 2]
        x0, x1 = jnp.concatenate([x0, x0], 1), jnp.concatenate([x1, x1], 1)
        r8 = iota((8, LANES), 0)
        message = jnp.where(r8 == 0, x0, jnp.where(r8 == 1, x1, 0.0))
        htx[...] = message
        hrx[c] = message
        each_other(n_bx, lambda d: copy4(lax.rem(c + d, n_bx), c).start())

    @pl.when(c < slots)
    def _():
        arrived((hrx.at[: slots - 1], r4))

    @pl.when(c >= slots)
    def _():
        arrived((hrx, r4))

    w_rows = 32
    r, l = iota((w_rows, LANES), 0), iota((w_rows, LANES), 1)
    coef = []
    for t in range(slots // 2):
        even, odd = (
            jnp.where(r % 2 == 0, hrx[2 * t + u, 0:1, :], hrx[2 * t + u, 1:2, :])
            for u in range(2)
        )
        tile = jnp.where((r // 2 == 2 * t) & (l < n_all), even, 0.0)
        coef.append(jnp.where((r // 2 == 2 * t + 1) & (l >= n_all), odd, tile).astype(bf16))
    coef = jnp.concatenate(coef, 1)

    tx3_rows = tx3.reshape(n_by, chunk, 2 * slots, LANES)

    def rebuild(p):
        x = jnp.concatenate([rows[p * chunk + n] for n in range(chunk)], 1)
        y = jnp.dot(coef, x, preferred_element_type=f32)[: 2 * slots].astype(bf16)
        for n in range(chunk):
            tx3_rows[p, n] = y[:, n * LANES : (n + 1) * LANES]

    def copy5(p, at):
        return pltpu.make_async_remote_copy(
            src_ref=tx3.at[p], dst_ref=rx3.at[:, at], send_sem=s5, recv_sem=r5,
            device_id={"by": p}, device_id_type=MESH,
        )

    def send5(d):
        p = lax.rem(j + d, n_by)
        rebuild(p)
        copy5(p, j).start()

    each_other(n_by, send5)
    rebuild(j)
    own5 = pltpu.make_async_copy(tx3.at[j], rx3.at[:, j], own_sem)
    own5.start()
    own5.wait()
    arrived((rx3.at[:, : n_by - 1], r5))

    rx3_rows = rx3.reshape(chunk, n_rows, LANES)
    tiles = [
        [
            jnp.dot(inverse, rx3_rows[k * per_comp + t], preferred_element_type=f32)
            .astype(bf16)
            .astype(f32)
            for t in range(per_comp)
        ]
        for k in range(n_comp)
    ]
    for s, tile in enumerate(split_groups(tiles, n_comp, n_bx, width)):
        tx4[s] = tile.astype(bf16)

    def copy6(p, at):
        return pltpu.make_async_remote_copy(
            src_ref=tx4.at[p], dst_ref=rx4.at[at], send_sem=s6, recv_sem=r6,
            device_id={"bx": p}, device_id_type=MESH,
        )

    each_other(n_bx, lambda d: copy6(lax.rem(c + d, n_bx), c).start())
    rx4[c] = tx4[c]
    arrived((rx4.at[: n_bx - 1], r6))
    merged = merge_groups(lambda s: rx4[s].astype(f32), n_comp, n_bx, width)
    for k in range(n_comp):
        for t in range(per_comp):
            out_ref[k, :, t * LANES : (t + 1) * LANES] = merged[k][t].astype(bf16)

    arrived(
        (tx1.at[: n_bx - 1], s1), (tx2.at[:, : (n_by - 1) * slots], s2),
        (tx3.at[: n_by - 1], s5), (tx4.at[: n_bx - 1], s6),
    )

    @pl.when(c < slots)
    def _():
        arrived((gtx.at[: slots - 1], s3), (hrx, s4), (hrx.at[: n_bx - 1 - slots], s4))

    @pl.when(c >= slots)
    def _():
        arrived((gtx, s3))


def local(snapshots, previous_block_coefficients, band_widths):
    n_time, n_comp, p_local = snapshots.shape
    n_bx = lax.axis_size("bx")
    n_by = lax.axis_size("by")
    slots, n_old = previous_block_coefficients.shape[:2]
    pairs = previous_block_coefficients.shape[-1]
    width = p_local // n_bx
    n_all = 2 * (n_old + 1)
    chunk = n_comp * p_local // LANES
    old = previous_block_coefficients.reshape(slots, n_old, 2, pairs // LANES, LANES)
    old = old.transpose(0, 1, 3, 2, 4)
    snap = snapshots.transpose(1, 0, 2)
    table_f, table_i = trig_constants(n_time)
    f32, bf16 = jnp.float32, jnp.bfloat16
    dma = pltpu.SemaphoreType.DMA
    vmem = pl.BlockSpec(memory_space=pltpu.VMEM)
    hbm = pl.BlockSpec(memory_space=pltpu.HBM)

    def body(*refs):
        kernel(n_bx, n_by, width, *refs)

    out = pl.pallas_call(
        body,
        out_shape=jax.ShapeDtypeStruct((n_comp, n_time, p_local), bf16),
        in_specs=[
            pl.BlockSpec(memory_space=pltpu.SMEM), hbm, hbm, hbm, hbm,
        ],
        out_specs=vmem,
        scratch_shapes=[
            pltpu.VMEM((n_comp, n_time, p_local), bf16),
            pltpu.VMEM(table_f.shape, bf16),
            pltpu.VMEM(table_i.shape, bf16),
            pltpu.VMEM((pairs // LANES, slots, n_all, LANES), bf16),
            pltpu.VMEM((slots, n_all, n_all), f32),
            pltpu.VMEM((n_bx, n_time, LANES), bf16),
            pltpu.VMEM((n_bx, n_time, LANES), bf16),
            pltpu.VMEM((chunk, n_by * slots, 2, LANES), bf16),
            pltpu.VMEM((slots, n_all // 2, LANES), f32),
            pltpu.VMEM((n_bx, n_all // 2, LANES), f32),
            pltpu.VMEM((8, LANES), f32),
            pltpu.VMEM((slots, 8, LANES), f32),
            pltpu.VMEM((n_by, chunk, slots, 2, LANES), bf16),
            pltpu.VMEM((chunk, n_by, slots, 2, LANES), bf16),
            pltpu.VMEM((n_bx, n_time, LANES), bf16),
            pltpu.VMEM((n_bx, n_time, LANES), bf16),
            dma, dma((2,)), dma((slots,)), dma,
            dma, dma, dma, dma((2, n_by)), dma, dma, dma, dma, dma, dma, dma, dma,
        ],
        compiler_params=pltpu.CompilerParams(
            collective_id=0, has_side_effects=True, vmem_limit_bytes=62 * 2**20
        ),
        cost_estimate=pl.CostEstimate(
            flops=4 * 10**9, bytes_accessed=20 * 10**6, transcendentals=0
        ),
    )(band_widths, jnp.asarray(table_f), jnp.asarray(table_i), snap, old)
    return out.transpose(1, 0, 2)


def solution(mesh):
    placed = (P(None, None, ("bx", "by")), P("by", None, None, "bx", None), P())
    return jax.shard_map(
        local, mesh=mesh, in_specs=placed, out_specs=P(None, None, ("bx", "by")), check_vma=False
    )
```

```python
import math

import jax
import jax.numpy as jnp
import ml_dtypes
import numpy as np
from jax import lax
from jax.experimental import pallas as pl
from jax.experimental.pallas import tpu as pltpu
from jax.sharding import PartitionSpec as P

MESH = pl.DeviceIdType.MESH
LANES = 128


def trig_constants(n_time):
    n_freq = n_time // 2 + 1
    freq = np.arange(n_freq, dtype=np.int32)
    times = np.arange(n_time, dtype=np.int32)
    turns = freq[:, None] * times % n_time
    angle = turns.astype(np.float32) * np.float32(2.0 * math.pi / n_time)
    window = np.float32(0.5) - np.float32(0.5) * np.cos(
        times.astype(np.float32) * np.float32(2.0 * math.pi / n_time)
    )
    factor = math.sqrt(8.0 / (3.0 * n_time))
    waves = np.stack([np.cos(angle), -np.sin(angle)], -2)
    forward = waves * (np.float32(factor) * window)
    weight = np.where((freq == 0) | (2 * freq == n_time), 1.0, 2.0) / (factor * n_time)
    inverse = waves * weight.astype(np.float32)[:, None, None]
    rows = 2 * n_freq
    table_f = np.zeros((LANES, n_time), np.float32)
    table_i = np.zeros((n_time, LANES), np.float32)
    table_f[:rows] = forward.reshape(rows, n_time)
    table_i[:, :rows] = inverse.reshape(rows, n_time).T
    return table_f.astype(ml_dtypes.bfloat16), table_i.astype(ml_dtypes.bfloat16)


def iota(shape, dim):
    return lax.broadcasted_iota(jnp.int32, shape, dim)


def place(acc, tile, dst, src, width, lane):
    shift = (dst - src) % LANES
    moved = pltpu.roll(tile, shift, 1) if shift else tile
    return jnp.where((lane >= dst) & (lane < dst + width), moved, acc)


def split_groups(tiles, n_comp, groups, width):
    shape = tiles[0][0].shape
    lane = iota(shape, 1)
    out = []
    for s in groups:
        acc = jnp.zeros(shape, tiles[0][0].dtype)
        for k in range(n_comp):
            a, done = s * width, 0
            while done < width:
                t, off = (a + done) // LANES, (a + done) % LANES
                n = min(width - done, LANES - off)
                acc = place(acc, tiles[k][t], k * width + done, off, n, lane)
                done += n
        out.append(acc)
    return out


def merge_groups(tile_of, n_comp, n_group, width):
    loaded = [tile_of(s) for s in range(n_group)]
    shape = loaded[0].shape
    lane = iota(shape, 1)
    out = []
    for k in range(n_comp):
        row = []
        for t in range(n_group * width // LANES):
            acc = jnp.zeros(shape, loaded[0].dtype)
            for s in range(t * LANES // width, (t * LANES + LANES - 1) // width + 1):
                lo = max(0, s * width - t * LANES)
                hi = min(LANES, (s + 1) * width - t * LANES)
                skip = lo - (s * width - t * LANES)
                acc = place(acc, loaded[s], lo, k * width + skip, hi - lo, lane)
            row.append(acc)
        out.append(row)
    return out


def kernel(
    n_bx, n_by, width,
    bw_ref, table_f_hbm, table_i_hbm, snap_hbm, old_ref, out_ref,
    snap_ref, table_f_ref, table_i_ref, buf, acc, tx1, rx1, tx2, gtx, grx, htx, hrx, tx3, rx3, tx4, rx4,
    snap_sem, table_sem, old_sem, own_sem, s1, r1, s2, r2, s3, r3, s4, r4, s5, r5, s6, r6,
):
    f32, bf16 = jnp.float32, jnp.bfloat16
    c, j = lax.axis_index("bx"), lax.axis_index("by")
    n_comp, n_time, p_local = snap_ref.shape
    slots, n_old = old_ref.shape[:2]
    n_all = 2 * (n_old + 1)
    per_comp = p_local // LANES
    chunk = n_comp * per_comp

    snap_copy = pltpu.make_async_copy(snap_hbm, snap_ref, snap_sem)
    snap_copy.start()
    table_copies = (
        pltpu.make_async_copy(table_f_hbm, table_f_ref, table_sem.at[0]),
        pltpu.make_async_copy(table_i_hbm, table_i_ref, table_sem.at[1]),
    )
    for copy in table_copies:
        copy.start()

    def each_other(n, fn):
        def step(d, carry):
            fn(d)
            return carry

        lax.fori_loop(1, n, step, 0)

    def arrived(*refs):
        for ref, sem in refs:
            pltpu.make_async_copy(ref, ref, sem).wait()

    barrier = pltpu.get_barrier_semaphore()

    def greet_bx(d, carry):
        pl.semaphore_signal(
            barrier, inc=1, device_id={"bx": lax.rem(c + d, n_bx)}, device_id_type=MESH
        )
        return carry

    def greet_by(d, carry):
        pl.semaphore_signal(
            barrier, inc=1, device_id={"by": lax.rem(j + d, n_by)}, device_id_type=MESH
        )
        return carry

    lax.fori_loop(1, n_bx, greet_bx, 0)
    lax.fori_loop(1, n_by, greet_by, 0)

    snap_copy.wait()
    tiles = [
        [snap_ref[k, :, t * LANES : (t + 1) * LANES] for t in range(per_comp)]
        for k in range(n_comp)
    ]
    for s, tile in enumerate(split_groups(tiles, n_comp, range(n_bx), width)):
        tx1[s] = tile

    pl.semaphore_wait(barrier, n_bx + n_by - 2)

    def copy1(p, at):
        return pltpu.make_async_remote_copy(
            src_ref=tx1.at[p], dst_ref=rx1.at[at], send_sem=s1, recv_sem=r1,
            device_id={"bx": p}, device_id_type=MESH,
        )

    def send1(d, carry):
        copy1(lax.rem(c + d, n_bx), c).start()
        return carry

    lax.fori_loop(1, n_bx, send1, 0)
    rx1[c] = tx1[c]

    def old_copy(f, b):
        return pltpu.make_async_copy(
            old_ref.at[f, b], buf.at[:, f, pl.ds(2 * b, 2)], old_sem.at[f]
        )

    def start_old(n, carry):
        old_copy(n // n_old, n % n_old).start()
        return carry

    lax.fori_loop(0, slots * n_old, start_old, 0)
    for copy in table_copies:
        copy.wait()

    n_rows = n_by * slots * 2
    row = iota((n_rows, LANES), 0)
    col = iota((n_rows, LANES), 1)
    band = row // (2 * slots)
    slot = (row // 2) % slots
    start = jnp.int32(0)
    wanted = jnp.full((n_rows, LANES), -1, jnp.int32)
    for b in range(n_by):
        w = bw_ref[b]
        wanted = jnp.where((band == b) & (slot < w), 2 * (start + slot) + row % 2, wanted)
        start = start + w
    pick = jnp.where(col == wanted, 1.0, 0.0).astype(bf16)
    forward = jnp.dot(pick, table_f_ref[...], preferred_element_type=f32).astype(bf16)
    inverse = lax.dot_general(
        table_i_ref[...], pick, (((1,), (1,)), ((), ())), preferred_element_type=f32
    ).astype(bf16)

    arrived((rx1.at[: n_bx - 1], r1))

    tx2_rows = tx2.reshape(chunk, n_rows, LANES)
    merged = merge_groups(lambda s: rx1[s], n_comp, n_bx, width)
    for k in range(n_comp):
        for t in range(per_comp):
            spectra = jnp.dot(forward, merged[k][t], preferred_element_type=f32)
            tx2_rows[k * per_comp + t] = spectra.astype(bf16)

    part = slots // 2

    def copy2(p, at, h):
        return pltpu.make_async_remote_copy(
            src_ref=tx2.at[:, pl.ds(p * slots + h * part, part)],
            dst_ref=buf.at[pl.ds(at * chunk, chunk), pl.ds(h * part, part), pl.ds(2 * n_old, 2)],
            send_sem=s2, recv_sem=r2.at[h, at],
            device_id={"by": p}, device_id_type=MESH,
        )

    for h in range(2):
        each_other(n_by, lambda d: copy2(lax.rem(j + d, n_by), j, h).start())
    own = pltpu.make_async_copy(
        tx2.at[:, pl.ds(j * slots, slots)],
        buf.at[pl.ds(j * chunk, chunk), :, pl.ds(2 * n_old, 2)],
        own_sem,
    )
    own.start()

    def wait_old(f, carry):
        whole = buf.at[:, f, pl.ds(0, 2 * n_old)]
        pltpu.make_async_copy(whole, whole, old_sem.at[f]).wait()
        return carry

    lax.fori_loop(0, slots, wait_old, 0)
    own.wait()

    rows = buf.reshape(n_by * chunk, slots * n_all, LANES)
    half = n_all // 2

    def gram(p, h, first):
        for f in range(h * part, (h + 1) * part):
            x = jnp.concatenate(
                [rows[p * chunk + l, f * n_all : (f + 1) * n_all, :] for l in range(chunk)], 1
            )
            g = lax.dot_general(x, x, (((1,), (1,)), ((), ())), preferred_element_type=f32)
            if first:
                acc[f] = g
            else:
                acc[f] += g

    def copy3(p, at):
        return pltpu.make_async_remote_copy(
            src_ref=gtx.at[p], dst_ref=grx.at[at], send_sem=s3, recv_sem=r3,
            device_id={"bx": p}, device_id_type=MESH,
        )

    for h in range(2):
        gram(j, h, True)

        def gram_step(d):
            p = lax.rem(j + n_by - d, n_by)
            copy2(j, p, h).wait_recv()
            gram(p, h, False)

        each_other(n_by, gram_step)
        for f in range(h * part, (h + 1) * part):
            g = acc[f]
            gtx[f] = jnp.concatenate([g[:half], g[half:]], 1)

        def send3(d):
            p = lax.rem(c + d, n_bx)

            @pl.when((p >= h * part) & (p < (h + 1) * part))
            def _():
                copy3(p, c).start()

        each_other(n_bx, send3)

    def copy4(p, at):
        return pltpu.make_async_remote_copy(
            src_ref=htx, dst_ref=hrx.at[at], send_sem=s4, recv_sem=r4,
            device_id={"bx": p}, device_id_type=MESH,
        )

    @pl.when(c < slots)
    def _():
        grx[c] = gtx[c]
        arrived((grx.at[: n_bx - 1], r3))
        total = grx[0]
        for i in range(1, n_bx):
            total = total + grx[i]
        prod = jnp.concatenate([total, pltpu.roll(total, half * 2, 1)], 0)
        shape = prod.shape
        r, l = iota(shape, 0), iota(shape, 1)
        prod = jnp.where(l < n_all, prod, 0.0)
        swap = jnp.where(r % 2 == 0, pltpu.roll(prod, n_all - 1, 0), pltpu.roll(prod, 1, 0))
        swap = jnp.where(l % 2 == 0, pltpu.roll(swap, LANES - 1, 1), pltpu.roll(swap, 1, 1))
        m = prod + jnp.where((r + l) % 2 == 0, swap, -swap)
        valid = c < bw_ref[j]
        m = jnp.where(valid, m, 0.0)
        diagonal = r == l
        shift = jnp.sum(jnp.where(diagonal, m, 0.0)) / n_all + jnp.where(valid, 0.0, 1.0)
        system = jnp.where(diagonal, m + shift, m)
        system = jnp.where(
            l < n_all, system, jnp.where(l < n_all + 2, pltpu.roll(m, 2, 1), 0.0)
        )
        for e in range(0, n_all, 4):
            column = [jnp.broadcast_to(system[:, e + n : e + n + 1], shape) for n in range(4)]
            top = [system[e + n : e + n + 1] for n in range(4)]
            a, b = column[0][e : e + 1], column[2][e + 2 : e + 3]
            u, w = column[2][e : e + 1], column[2][e + 1 : e + 2]
            inv = 1.0 / (a * b - (u * u + w * w))
            new = [
                (b * top[0] - u * top[2] + w * top[3]) * inv,
                (b * top[1] - w * top[2] - u * top[3]) * inv,
                (a * top[2] - u * top[0] - w * top[1]) * inv,
                (a * top[3] + w * top[0] - u * top[1]) * inv,
            ]
            left = system - (column[0] * new[0] + column[1] * new[1])
            left = left - (column[2] * new[2] + column[3] * new[3])
            for n in range(4):
                left = jnp.where(r == e + n, new[n], left)
            system = left
        turned = jnp.transpose(system)
        x0, x1 = turned[n_all : n_all + 1], turned[n_all + 1 : n_all + 2]
        x0, x1 = jnp.concatenate([x0, x0], 1), jnp.concatenate([x1, x1], 1)
        r8 = iota((8, LANES), 0)
        message = jnp.where(r8 == 0, x0, jnp.where(r8 == 1, x1, 0.0))
        htx[...] = message
        hrx[c] = message
        each_other(n_bx, lambda d: copy4(lax.rem(c + d, n_bx), c).start())

    @pl.when(c < slots)
    def _():
        arrived((hrx.at[: slots - 1], r4))

    @pl.when(c >= slots)
    def _():
        arrived((hrx, r4))

    w_rows = 32
    r, l = iota((w_rows, LANES), 0), iota((w_rows, LANES), 1)
    coef = []
    for t in range(slots // 2):
        even, odd = (
            jnp.where(r % 2 == 0, hrx[2 * t + u, 0:1, :], hrx[2 * t + u, 1:2, :])
            for u in range(2)
        )
        tile = jnp.where((r // 2 == 2 * t) & (l < n_all), even, 0.0)
        coef.append(jnp.where((r // 2 == 2 * t + 1) & (l >= n_all), odd, tile).astype(bf16))
    coef = jnp.concatenate(coef, 1)

    tx3_rows = tx3.reshape(n_by, chunk, 2 * slots, LANES)

    def rebuild(p):
        x = jnp.concatenate([rows[p * chunk + n] for n in range(chunk)], 1)
        y = jnp.dot(coef, x, preferred_element_type=f32)[: 2 * slots].astype(bf16)
        for n in range(chunk):
            tx3_rows[p, n] = y[:, n * LANES : (n + 1) * LANES]

    def copy5(p, at):
        return pltpu.make_async_remote_copy(
            src_ref=tx3.at[p], dst_ref=rx3.at[:, at], send_sem=s5, recv_sem=r5,
            device_id={"by": p}, device_id_type=MESH,
        )

    def send5(d):
        p = lax.rem(j + d, n_by)
        rebuild(p)
        copy5(p, j).start()

    each_other(n_by, send5)
    rebuild(j)
    own5 = pltpu.make_async_copy(tx3.at[j], rx3.at[:, j], own_sem)
    own5.start()
    own5.wait()
    arrived((rx3.at[:, : n_by - 1], r5))

    rx3_rows = rx3.reshape(chunk, n_rows, LANES)
    tiles = [
        [
            jnp.dot(inverse, rx3_rows[k * per_comp + t], preferred_element_type=f32)
            .astype(bf16)
            for t in range(per_comp)
        ]
        for k in range(n_comp)
    ]
    for s, tile in enumerate(split_groups(tiles, n_comp, range(n_bx), width)):
        tx4[s] = tile

    def copy6(p, at):
        return pltpu.make_async_remote_copy(
            src_ref=tx4.at[p], dst_ref=rx4.at[at], send_sem=s6, recv_sem=r6,
            device_id={"bx": p}, device_id_type=MESH,
        )

    each_other(n_bx, lambda d: copy6(lax.rem(c + d, n_bx), c).start())
    rx4[c] = tx4[c]
    arrived((rx4.at[: n_bx - 1], r6))
    merged = merge_groups(lambda s: rx4[s], n_comp, n_bx, width)
    for k in range(n_comp):
        for t in range(per_comp):
            out_ref[k, :, t * LANES : (t + 1) * LANES] = merged[k][t]

    arrived(
        (tx1.at[: n_bx - 1], s1), (tx2.at[:, : (n_by - 1) * slots], s2),
        (tx3.at[: n_by - 1], s5), (tx4.at[: n_bx - 1], s6),
    )

    @pl.when(c < slots)
    def _():
        arrived((gtx.at[: slots - 1], s3), (hrx, s4), (hrx.at[: n_bx - 1 - slots], s4))

    @pl.when(c >= slots)
    def _():
        arrived((gtx, s3))


def local(snapshots, previous_block_coefficients, band_widths):
    n_time, n_comp, p_local = snapshots.shape
    n_bx = lax.axis_size("bx")
    n_by = lax.axis_size("by")
    slots, n_old = previous_block_coefficients.shape[:2]
    pairs = previous_block_coefficients.shape[-1]
    width = p_local // n_bx
    n_all = 2 * (n_old + 1)
    chunk = n_comp * p_local // LANES
    old = previous_block_coefficients.reshape(slots, n_old, 2, pairs // LANES, LANES)
    old = old.transpose(0, 1, 3, 2, 4)
    snap = snapshots.transpose(1, 0, 2)
    table_f, table_i = trig_constants(n_time)
    f32, bf16 = jnp.float32, jnp.bfloat16
    dma = pltpu.SemaphoreType.DMA
    vmem = pl.BlockSpec(memory_space=pltpu.VMEM)
    hbm = pl.BlockSpec(memory_space=pltpu.HBM)

    def body(*refs):
        kernel(n_bx, n_by, width, *refs)

    out = pl.pallas_call(
        body,
        out_shape=jax.ShapeDtypeStruct((n_comp, n_time, p_local), bf16),
        in_specs=[
            pl.BlockSpec(memory_space=pltpu.SMEM), hbm, hbm, hbm, hbm,
        ],
        out_specs=vmem,
        scratch_shapes=[
            pltpu.VMEM((n_comp, n_time, p_local), bf16),
            pltpu.VMEM(table_f.shape, bf16),
            pltpu.VMEM(table_i.shape, bf16),
            pltpu.VMEM((pairs // LANES, slots, n_all, LANES), bf16),
            pltpu.VMEM((slots, n_all, n_all), f32),
            pltpu.VMEM((n_bx, n_time, LANES), bf16),
            pltpu.VMEM((n_bx, n_time, LANES), bf16),
            pltpu.VMEM((chunk, n_by * slots, 2, LANES), bf16),
            pltpu.VMEM((slots, n_all // 2, LANES), f32),
            pltpu.VMEM((n_bx, n_all // 2, LANES), f32),
            pltpu.VMEM((8, LANES), f32),
            pltpu.VMEM((slots, 8, LANES), f32),
            pltpu.VMEM((n_by, chunk, slots, 2, LANES), bf16),
            pltpu.VMEM((chunk, n_by, slots, 2, LANES), bf16),
            pltpu.VMEM((n_bx, n_time, LANES), bf16),
            pltpu.VMEM((n_bx, n_time, LANES), bf16),
            dma, dma((2,)), dma((slots,)), dma,
            dma, dma, dma, dma((2, n_by)), dma, dma, dma, dma, dma, dma, dma, dma,
        ],
        compiler_params=pltpu.CompilerParams(
            collective_id=0, has_side_effects=True, vmem_limit_bytes=62 * 2**20
        ),
        cost_estimate=pl.CostEstimate(
            flops=4 * 10**9, bytes_accessed=20 * 10**6, transcendentals=0
        ),
    )(band_widths, jnp.asarray(table_f), jnp.asarray(table_i), snap, old)
    return out.transpose(1, 0, 2)


def solution(mesh):
    placed = (P(None, None, ("bx", "by")), P("by", None, None, "bx", None), P())
    return jax.shard_map(
        local, mesh=mesh, in_specs=placed, out_specs=P(None, None, ("bx", "by")), check_vma=False
    )
```

```python
import math

import jax
import jax.numpy as jnp
import ml_dtypes
import numpy as np
from jax import lax
from jax.experimental import pallas as pl
from jax.experimental.pallas import tpu as pltpu
from jax.sharding import PartitionSpec as P

MESH = pl.DeviceIdType.MESH
LANES = 128


def trig_constants(n_time):
    n_freq = n_time // 2 + 1
    freq = np.arange(n_freq, dtype=np.int32)
    times = np.arange(n_time, dtype=np.int32)
    turns = freq[:, None] * times % n_time
    angle = turns.astype(np.float32) * np.float32(2.0 * math.pi / n_time)
    window = np.float32(0.5) - np.float32(0.5) * np.cos(
        times.astype(np.float32) * np.float32(2.0 * math.pi / n_time)
    )
    factor = math.sqrt(8.0 / (3.0 * n_time))
    waves = np.stack([np.cos(angle), -np.sin(angle)], -2)
    forward = waves * (np.float32(factor) * window)
    weight = np.where((freq == 0) | (2 * freq == n_time), 1.0, 2.0) / (factor * n_time)
    inverse = waves * weight.astype(np.float32)[:, None, None]
    rows = 2 * n_freq
    table_f = np.zeros((LANES, n_time), np.float32)
    table_i = np.zeros((n_time, LANES), np.float32)
    table_f[:rows] = forward.reshape(rows, n_time)
    table_i[:, :rows] = inverse.reshape(rows, n_time).T
    return table_f.astype(ml_dtypes.bfloat16), table_i.astype(ml_dtypes.bfloat16)


def iota(shape, dim):
    return lax.broadcasted_iota(jnp.int32, shape, dim)


def place(acc, tile, dst, src, width, lane):
    shift = (dst - src) % LANES
    moved = pltpu.roll(tile, shift, 1) if shift else tile
    return jnp.where((lane >= dst) & (lane < dst + width), moved, acc)


def split_groups(tiles, n_comp, groups, width):
    shape = tiles[0][0].shape
    lane = iota(shape, 1)
    out = []
    for s in groups:
        acc = jnp.zeros(shape, tiles[0][0].dtype)
        for k in range(n_comp):
            a, done = s * width, 0
            while done < width:
                t, off = (a + done) // LANES, (a + done) % LANES
                n = min(width - done, LANES - off)
                acc = place(acc, tiles[k][t], k * width + done, off, n, lane)
                done += n
        out.append(acc)
    return out


def merge_groups(tile_of, n_comp, n_group, width):
    loaded = [tile_of(s) for s in range(n_group)]
    shape = loaded[0].shape
    lane = iota(shape, 1)
    out = []
    for k in range(n_comp):
        row = []
        for t in range(n_group * width // LANES):
            acc = jnp.zeros(shape, loaded[0].dtype)
            for s in range(t * LANES // width, (t * LANES + LANES - 1) // width + 1):
                lo = max(0, s * width - t * LANES)
                hi = min(LANES, (s + 1) * width - t * LANES)
                skip = lo - (s * width - t * LANES)
                acc = place(acc, loaded[s], lo, k * width + skip, hi - lo, lane)
            row.append(acc)
        out.append(row)
    return out


def kernel(
    n_bx, n_by, width,
    bw_ref, table_f_hbm, table_i_hbm, snap_hbm, old_ref, out_ref,
    snap_ref, table_f_ref, table_i_ref, buf, acc, tx1, rx1, tx2, gtx, grx, htx, hrx, tx3, rx3, tx4, rx4,
    snap_sem, table_sem, old_sem, own_sem, s1, r1, s2, r2, s3, r3, s4, r4, s5, r5, s6, r6,
):
    f32, bf16 = jnp.float32, jnp.bfloat16
    c, j = lax.axis_index("bx"), lax.axis_index("by")
    n_comp, n_time, p_local = snap_ref.shape
    slots, n_old = old_ref.shape[:2]
    n_all = 2 * (n_old + 1)
    per_comp = p_local // LANES
    chunk = n_comp * per_comp

    snap_copy = pltpu.make_async_copy(snap_hbm, snap_ref, snap_sem)
    snap_copy.start()
    table_copies = (
        pltpu.make_async_copy(table_f_hbm, table_f_ref, table_sem.at[0]),
        pltpu.make_async_copy(table_i_hbm, table_i_ref, table_sem.at[1]),
    )
    for copy in table_copies:
        copy.start()

    def each_other(n, fn):
        def step(d, carry):
            fn(d)
            return carry

        lax.fori_loop(1, n, step, 0)

    def arrived(*refs):
        for ref, sem in refs:
            pltpu.make_async_copy(ref, ref, sem).wait()

    barrier = pltpu.get_barrier_semaphore()

    def greet_bx(d, carry):
        pl.semaphore_signal(
            barrier, inc=1, device_id={"bx": lax.rem(c + d, n_bx)}, device_id_type=MESH
        )
        return carry

    def greet_by(d, carry):
        pl.semaphore_signal(
            barrier, inc=1, device_id={"by": lax.rem(j + d, n_by)}, device_id_type=MESH
        )
        return carry

    lax.fori_loop(1, n_bx, greet_bx, 0)
    lax.fori_loop(1, n_by, greet_by, 0)

    acc[...] = jnp.zeros_like(acc)
    snap_copy.wait()
    tiles = [
        [snap_ref[k, :, t * LANES : (t + 1) * LANES] for t in range(per_comp)]
        for k in range(n_comp)
    ]
    for s, tile in enumerate(split_groups(tiles, n_comp, range(n_bx), width)):
        tx1[s] = tile

    pl.semaphore_wait(barrier, n_bx + n_by - 2)

    def copy1(p, at):
        return pltpu.make_async_remote_copy(
            src_ref=tx1.at[p], dst_ref=rx1.at[at], send_sem=s1, recv_sem=r1,
            device_id={"bx": p}, device_id_type=MESH,
        )

    def send1(d, carry):
        copy1(lax.rem(c + d, n_bx), c).start()
        return carry

    lax.fori_loop(1, n_bx, send1, 0)
    rx1[c] = tx1[c]

    def old_copy(f, b):
        return pltpu.make_async_copy(
            old_ref.at[f, b], buf.at[:, f, pl.ds(2 * b, 2)], old_sem.at[f]
        )

    def start_old(n, carry):
        old_copy(n // n_old, n % n_old).start()
        return carry

    lax.fori_loop(0, slots * n_old, start_old, 0)
    for copy in table_copies:
        copy.wait()

    n_rows = n_by * slots * 2
    row = iota((n_rows, LANES), 0)
    col = iota((n_rows, LANES), 1)
    band = row // (2 * slots)
    slot = (row // 2) % slots
    start = jnp.int32(0)
    wanted = jnp.full((n_rows, LANES), -1, jnp.int32)
    for b in range(n_by):
        w = bw_ref[b]
        wanted = jnp.where((band == b) & (slot < w), 2 * (start + slot) + row % 2, wanted)
        start = start + w
    pick = jnp.where(col == wanted, 1.0, 0.0).astype(bf16)
    forward = jnp.dot(pick, table_f_ref[...], preferred_element_type=f32).astype(bf16)
    inverse = lax.dot_general(
        table_i_ref[...], pick, (((1,), (1,)), ((), ())), preferred_element_type=f32
    ).astype(bf16)

    arrived((rx1.at[: n_bx - 1], r1))

    tx2_rows = tx2.reshape(chunk, n_rows, LANES)
    merged = merge_groups(lambda s: rx1[s], n_comp, n_bx, width)
    for k in range(n_comp):
        for t in range(per_comp):
            spectra = jnp.dot(forward, merged[k][t], preferred_element_type=f32)
            tx2_rows[k * per_comp + t] = spectra.astype(bf16)

    part = slots // 2

    def copy2(p, at, h):
        return pltpu.make_async_remote_copy(
            src_ref=tx2.at[:, pl.ds(p * slots + h * part, part)],
            dst_ref=buf.at[pl.ds(at * chunk, chunk), pl.ds(h * part, part), pl.ds(2 * n_old, 2)],
            send_sem=s2, recv_sem=r2.at[h, at],
            device_id={"by": p}, device_id_type=MESH,
        )

    for h in range(2):
        each_other(n_by, lambda d: copy2(lax.rem(j + d, n_by), j, h).start())
    own = pltpu.make_async_copy(
        tx2.at[:, pl.ds(j * slots, slots)],
        buf.at[pl.ds(j * chunk, chunk), :, pl.ds(2 * n_old, 2)],
        own_sem,
    )
    own.start()

    def wait_old(f, carry):
        whole = buf.at[:, f, pl.ds(0, 2 * n_old)]
        pltpu.make_async_copy(whole, whole, old_sem.at[f]).wait()
        return carry

    lax.fori_loop(0, slots, wait_old, 0)
    own.wait()

    rows = buf.reshape(n_by * chunk, slots * n_all, LANES)
    half = n_all // 2
    g_row, g_col = iota((n_all, LANES), 0), iota((n_all, LANES), 1)

    def swap_lanes(x, step):
        return pltpu.roll(x, (LANES - step) % LANES, 1)

    def gram(p, h, first):
        for f in range(h * part, (h + 1) * part):
            x = jnp.concatenate(
                [rows[p * chunk + l, f * n_all : (f + 1) * n_all, :] for l in range(chunk)], 1
            )
            g = lax.dot_general(x, x, (((1,), (1,)), ((), ())), preferred_element_type=f32)
            if first:
                acc[f, :, :n_all] = g
            else:
                acc[f, :, :n_all] += g

    def copy3(p, at):
        return pltpu.make_async_remote_copy(
            src_ref=gtx.at[p], dst_ref=grx.at[at], send_sem=s3, recv_sem=r3,
            device_id={"bx": p}, device_id_type=MESH,
        )

    for h in range(2):
        gram(j, h, True)

        def gram_step(d):
            p = lax.rem(j + n_by - d, n_by)
            copy2(j, p, h).wait_recv()
            gram(p, h, False)

        each_other(n_by, gram_step)
        for f in range(h * part, (h + 1) * part):
            g = acc[f]
            swap = jnp.where(g_row % 2 == 0, pltpu.roll(g, n_all - 1, 0), pltpu.roll(g, 1, 0))
            swap = jnp.where(g_col % 2 == 0, swap_lanes(swap, 1), swap_lanes(swap, -1))
            acc[f] = jnp.where((g_row + g_col) % 2 == 0, g + swap, g - swap)
            even = acc[f, pl.ds(0, half, stride=2), :]
            gtx[f] = jnp.where(
                g_col[: half // 2] < n_all,
                even[: half // 2],
                pltpu.roll(even[half // 2 :], n_all, 1),
            )

        def send3(d):
            p = lax.rem(c + d, n_bx)

            @pl.when((p >= h * part) & (p < (h + 1) * part))
            def _():
                copy3(p, c).start()

        each_other(n_bx, send3)

    def copy4(p, at):
        return pltpu.make_async_remote_copy(
            src_ref=htx, dst_ref=hrx.at[at], send_sem=s4, recv_sem=r4,
            device_id={"bx": p}, device_id_type=MESH,
        )

    @pl.when(c < slots)
    def _():
        grx[c] = gtx[c]
        arrived((grx.at[: n_bx - 1], r3))
        total = grx[0]
        for i in range(1, n_bx):
            total = total + grx[i]
        even = jnp.concatenate([total, pltpu.roll(total, n_all, 1)], 0)
        e_col = g_col[:half]
        odd = jnp.where(e_col % 2 == 0, -swap_lanes(even, 1), swap_lanes(even, -1))
        acc[0, pl.ds(0, half, stride=2), :] = even
        acc[0, pl.ds(1, half, stride=2), :] = odd
        r, l = g_row, g_col
        shape = r.shape
        m = jnp.where(l < n_all, acc[0], 0.0)
        valid = c < bw_ref[j]
        m = jnp.where(valid, m, 0.0)
        diagonal = r == l
        shift = jnp.sum(jnp.where(diagonal, m, 0.0)) / n_all + jnp.where(valid, 0.0, 1.0)
        system = jnp.where(diagonal, m + shift, m)
        system = jnp.where(
            l < n_all, system, jnp.where(l < n_all + 2, pltpu.roll(m, 2, 1), 0.0)
        )
        for e in range(0, n_all, 4):
            column = [jnp.broadcast_to(system[:, e + n : e + n + 1], shape) for n in range(4)]
            top = [system[e + n : e + n + 1] for n in range(4)]
            a, b = column[0][e : e + 1], column[2][e + 2 : e + 3]
            u, w = column[2][e : e + 1], column[2][e + 1 : e + 2]
            inv = 1.0 / (a * b - (u * u + w * w))
            new = [
                (b * top[0] - u * top[2] + w * top[3]) * inv,
                (b * top[1] - w * top[2] - u * top[3]) * inv,
                (a * top[2] - u * top[0] - w * top[1]) * inv,
                (a * top[3] + w * top[0] - u * top[1]) * inv,
            ]
            left = system - (column[0] * new[0] + column[1] * new[1])
            left = left - (column[2] * new[2] + column[3] * new[3])
            for n in range(4):
                left = jnp.where(r == e + n, new[n], left)
            system = left
        turned = jnp.transpose(system)
        x0, x1 = turned[n_all : n_all + 1], turned[n_all + 1 : n_all + 2]
        x0, x1 = jnp.concatenate([x0, x0], 1), jnp.concatenate([x1, x1], 1)
        r8 = iota((8, LANES), 0)
        message = jnp.where(r8 == 0, x0, jnp.where(r8 == 1, x1, 0.0))
        htx[...] = message
        hrx[c] = message
        each_other(n_bx, lambda d: copy4(lax.rem(c + d, n_bx), c).start())

    @pl.when(c < slots)
    def _():
        arrived((hrx.at[: slots - 1], r4))

    @pl.when(c >= slots)
    def _():
        arrived((hrx, r4))

    w_rows = 32
    r, l = iota((w_rows, LANES), 0), iota((w_rows, LANES), 1)
    coef = []
    for t in range(slots // 2):
        even, odd = (
            jnp.where(r % 2 == 0, hrx[2 * t + u, 0:1, :], hrx[2 * t + u, 1:2, :])
            for u in range(2)
        )
        tile = jnp.where((r // 2 == 2 * t) & (l < n_all), even, 0.0)
        coef.append(jnp.where((r // 2 == 2 * t + 1) & (l >= n_all), odd, tile).astype(bf16))
    coef = jnp.concatenate(coef, 1)

    tx3_rows = tx3.reshape(n_by, chunk, 2 * slots, LANES)

    def rebuild(p):
        x = jnp.concatenate([rows[p * chunk + n] for n in range(chunk)], 1)
        y = jnp.dot(coef, x, preferred_element_type=f32)[: 2 * slots].astype(bf16)
        for n in range(chunk):
            tx3_rows[p, n] = y[:, n * LANES : (n + 1) * LANES]

    def copy5(p, at):
        return pltpu.make_async_remote_copy(
            src_ref=tx3.at[p], dst_ref=rx3.at[:, at], send_sem=s5, recv_sem=r5,
            device_id={"by": p}, device_id_type=MESH,
        )

    def send5(d):
        p = lax.rem(j + d, n_by)
        rebuild(p)
        copy5(p, j).start()

    each_other(n_by, send5)
    rebuild(j)
    own5 = pltpu.make_async_copy(tx3.at[j], rx3.at[:, j], own_sem)
    own5.start()
    own5.wait()
    arrived((rx3.at[:, : n_by - 1], r5))

    rx3_rows = rx3.reshape(chunk, n_rows, LANES)
    tiles = [
        [
            jnp.dot(inverse, rx3_rows[k * per_comp + t], preferred_element_type=f32)
            .astype(bf16)
            for t in range(per_comp)
        ]
        for k in range(n_comp)
    ]
    for s, tile in enumerate(split_groups(tiles, n_comp, range(n_bx), width)):
        tx4[s] = tile

    def copy6(p, at):
        return pltpu.make_async_remote_copy(
            src_ref=tx4.at[p], dst_ref=rx4.at[at], send_sem=s6, recv_sem=r6,
            device_id={"bx": p}, device_id_type=MESH,
        )

    each_other(n_bx, lambda d: copy6(lax.rem(c + d, n_bx), c).start())
    rx4[c] = tx4[c]
    arrived((rx4.at[: n_bx - 1], r6))
    merged = merge_groups(lambda s: rx4[s], n_comp, n_bx, width)
    for k in range(n_comp):
        for t in range(per_comp):
            out_ref[k, :, t * LANES : (t + 1) * LANES] = merged[k][t]

    arrived(
        (tx1.at[: n_bx - 1], s1), (tx2.at[:, : (n_by - 1) * slots], s2),
        (tx3.at[: n_by - 1], s5), (tx4.at[: n_bx - 1], s6),
    )

    @pl.when(c < slots)
    def _():
        arrived((gtx.at[: slots - 1], s3), (hrx, s4), (hrx.at[: n_bx - 1 - slots], s4))

    @pl.when(c >= slots)
    def _():
        arrived((gtx, s3))


def local(snapshots, previous_block_coefficients, band_widths):
    n_time, n_comp, p_local = snapshots.shape
    n_bx = lax.axis_size("bx")
    n_by = lax.axis_size("by")
    slots, n_old = previous_block_coefficients.shape[:2]
    pairs = previous_block_coefficients.shape[-1]
    width = p_local // n_bx
    n_all = 2 * (n_old + 1)
    chunk = n_comp * p_local // LANES
    old = previous_block_coefficients.reshape(slots, n_old, 2, pairs // LANES, LANES)
    old = old.transpose(0, 1, 3, 2, 4)
    snap = snapshots.transpose(1, 0, 2)
    table_f, table_i = trig_constants(n_time)
    f32, bf16 = jnp.float32, jnp.bfloat16
    dma = pltpu.SemaphoreType.DMA
    vmem = pl.BlockSpec(memory_space=pltpu.VMEM)
    hbm = pl.BlockSpec(memory_space=pltpu.HBM)

    def body(*refs):
        kernel(n_bx, n_by, width, *refs)

    out = pl.pallas_call(
        body,
        out_shape=jax.ShapeDtypeStruct((n_comp, n_time, p_local), bf16),
        in_specs=[
            pl.BlockSpec(memory_space=pltpu.SMEM), hbm, hbm, hbm, hbm,
        ],
        out_specs=vmem,
        scratch_shapes=[
            pltpu.VMEM((n_comp, n_time, p_local), bf16),
            pltpu.VMEM(table_f.shape, bf16),
            pltpu.VMEM(table_i.shape, bf16),
            pltpu.VMEM((pairs // LANES, slots, n_all, LANES), bf16),
            pltpu.VMEM((slots, n_all, LANES), f32),
            pltpu.VMEM((n_bx, n_time, LANES), bf16),
            pltpu.VMEM((n_bx, n_time, LANES), bf16),
            pltpu.VMEM((chunk, n_by * slots, 2, LANES), bf16),
            pltpu.VMEM((slots, n_all // 4, LANES), f32),
            pltpu.VMEM((n_bx, n_all // 4, LANES), f32),
            pltpu.VMEM((8, LANES), f32),
            pltpu.VMEM((slots, 8, LANES), f32),
            pltpu.VMEM((n_by, chunk, slots, 2, LANES), bf16),
            pltpu.VMEM((chunk, n_by, slots, 2, LANES), bf16),
            pltpu.VMEM((n_bx, n_time, LANES), bf16),
            pltpu.VMEM((n_bx, n_time, LANES), bf16),
            dma, dma((2,)), dma((slots,)), dma,
            dma, dma, dma, dma((2, n_by)), dma, dma, dma, dma, dma, dma, dma, dma,
        ],
        compiler_params=pltpu.CompilerParams(
            collective_id=0, has_side_effects=True, vmem_limit_bytes=62 * 2**20
        ),
        cost_estimate=pl.CostEstimate(
            flops=4 * 10**9, bytes_accessed=20 * 10**6, transcendentals=0
        ),
    )(band_widths, jnp.asarray(table_f), jnp.asarray(table_i), snap, old)
    return out.transpose(1, 0, 2)


def solution(mesh):
    placed = (P(None, None, ("bx", "by")), P("by", None, None, "bx", None), P())
    return jax.shard_map(
        local, mesh=mesh, in_specs=placed, out_specs=P(None, None, ("bx", "by")), check_vma=False
    )
```
